32 devices in a mesh: dp: 8 (over z, x), tensor: 4 (over y, core).
Axes of the slice: x: 2, y: 2, z: 4, core: 2. Of those that a mesh axis runs over, the one named last changes fastest.
Arguments:
- activations: bfloat16 [4096, 16384], P('dp', 'tensor'), may hold values from -40 to 40, as said below
- token_ids: int32 [4096], P('dp'), may hold values from 0 to 128004, as said below
- weight: bfloat16 [16384, 16384], P('dp', 'tensor'), may hold values from -6 to 6
- inv_chol: float32 [128, 128, 1024], P('tensor', 'dp'), may hold values from -1 to 2, as said below
- bit_widths: int32 [128], P('tensor'), may hold values from 2 to 8, as said below
Outputs:
- quantized: bfloat16 [16384, 16384], P('dp', 'tensor')
- gram_blocks: float32 [128, 128, 128], P('tensor', 'dp')
- block_errors: float32 [128, 4], replicated
The draws below stay inside these ranges and needn't reach their ends.
Inputs may be any that keep to these rules, and one draw needn't show every extreme that they name: `token_ids`: id 128004 marks padding. In the d-th aligned block of 512 tokens (d = 0 .. 7), exactly 170 + d*342//7 tokens are not padding, at positions drawn from the seed; the last block has no padding. `bit_widths`: each entry is 2, 3, 4 or 8. `inv_chol`: row i of block b, with j = b mod (8), holds a positive entry at column j*128+i, arbitrary entries at columns from (j+1)*128 on, and zeros elsewhere. `activations`: finite values.
All inputs are finite; a program needn't handle non-finite values.
Results may differ from the reference program's by a relative error of at most 0.001.
Values sent between devices are 32-bit elements; how exact they have to be, the bound alone decides.
A program may use at most 192 MiB of HBM per device.

```python
import math
import jax
import jax.numpy as jnp
from jax import lax

D = 16384
OUT = 16384
BLK = 128
PANEL = 1024
TOK_DEV = 512
TOKENS = 4096
BLOCKS = 128


def draw_activations(key, part):
    first_key, second_key, third_key = jax.random.split(key, 3)
    row_scale = jnp.exp(jax.random.uniform(second_key, (TOKENS, 1), jnp.float32, math.log(0.3), math.log(3.0)))
    column_scale = jnp.exp(jax.random.uniform(third_key, (1, D), jnp.float32, math.log(0.5), math.log(2.0)))
    normal_part = jax.random.normal(first_key, (TOKENS, D), jnp.float32)
    return jnp.clip(normal_part * row_scale * column_scale, -40.0, 40.0).astype(jnp.bfloat16)


def draw_token_ids(key, part):
    block_count = TOKENS // TOK_DEV
    first_key, second_key = jax.random.split(key)
    fewest_live = TOK_DEV // 3
    live_counts = fewest_live + jnp.arange(block_count, dtype=jnp.int32) * (TOK_DEV - fewest_live) // max(block_count - 1, 1)
    block_keys = jax.random.split(second_key, block_count)
    position_rank = jax.vmap(lambda one_key: jax.random.permutation(one_key, TOK_DEV))(block_keys)
    word_ids = jax.random.randint(first_key, (block_count, TOK_DEV), 0, 128000)
    chosen = jnp.where(position_rank < live_counts[:, None], word_ids, 128004)
    return chosen.reshape(TOKENS).astype(jnp.int32)


def draw_inv_chol(key, part):
    per_panel = PANEL // BLK
    first_key, second_key = jax.random.split(key)
    block_index = jnp.arange(BLOCKS)[:, None, None] % per_panel
    row_index = jnp.arange(BLK)[None, :, None]
    column = jnp.arange(PANEL)[None, None, :]
    on_diagonal = column == block_index * BLK + row_index
    beyond = column >= (block_index + 1) * BLK
    diagonal_values = jnp.exp(jax.random.uniform(first_key, (BLOCKS, BLK, PANEL), jnp.float32, math.log(0.5), math.log(2.0)))
    spread = jnp.clip(jax.random.normal(second_key, (BLOCKS, BLK, PANEL), jnp.float32), -4.0, 4.0) * (0.5 / math.sqrt(PANEL))
    return jnp.where(on_diagonal, diagonal_values, jnp.where(beyond, spread, 0.0)).astype(jnp.float32)


def draw_bit_widths(key, part):
    width_index = jax.random.randint(key, (BLOCKS,), 0, 4)
    return jnp.where(width_index == 0, 2, jnp.where(width_index == 1, 3, jnp.where(width_index == 2, 4, 8))).astype(jnp.int32)


def block_levels(rng, dims, shards, smallest, high):
    loudness = 1.0
    for dim, parts in shards:
        steps = jax.random.uniform(jax.random.fold_in(jax.random.fold_in(rng, 6), dim), (parts,), jnp.float32, smallest / len(shards), high / len(shards))
        loudness = loudness * jnp.repeat(jnp.exp(steps), dims[dim] // parts).reshape((-1,) + (1,) * (len(dims) - 1 - dim))
    return loudness


def noise(rng, extent, width, reach, shards=(), kind=jnp.bfloat16):
    entries = jax.random.normal(rng, extent, jnp.float32) * width
    if len(shards) > 0:
        entries = block_levels(rng, extent, shards, -0.22, 0.18) * entries
    return jnp.clip(entries, min=-reach, max=reach).astype(kind)


def setup_inputs(seed: int = 0) -> dict:
    splits = jax.random.split(jax.random.key(seed), 6)
    activations = draw_activations(jax.random.fold_in(splits[5], 71), 0)
    token_ids = draw_token_ids(jax.random.fold_in(splits[5], 71), 0)
    weight = noise(splits[2], (OUT, D), 1.0, 6.0, ((0, 8), (1, 4)))
    inv_chol = draw_inv_chol(jax.random.fold_in(splits[5], 71), 0)
    bit_widths = draw_bit_widths(jax.random.fold_in(splits[5], 71), 0)
    return {"activations": activations, "token_ids": token_ids, "weight": weight, "inv_chol": inv_chol, "bit_widths": bit_widths}


pad_token = 128004


def level_count(widths):
    return jnp.where(widths == 2, 2.0, jnp.where(widths == 3, 4.0, jnp.where(widths == 4, 8.0, 128.0))).astype(jnp.float32)


def soft_quantize(values, levels):
    largest = jnp.max(jnp.abs(values), axis=-1, keepdims=True)
    step_size = (largest + 1e-6) / (levels - 0.5)
    scaled = values / step_size
    smooth = scaled - jnp.sin(2.0 * jnp.pi * scaled) / (2.0 * jnp.pi)
    return step_size * jnp.clip(smooth, -levels, levels - 1.0)


def reference(activations, token_ids, weight, inv_chol, bit_widths):
    live = (token_ids != pad_token).astype(jnp.float32)
    count = jnp.sum(live)
    stacked = activations.reshape(TOKENS, BLOCKS, BLK).transpose(1, 0, 2)
    live_rows = live.astype(activations.dtype)[:, None]

    def block_gram(block_piece):
        return jnp.dot((block_piece * live_rows).T, block_piece, preferred_element_type=jnp.float32)

    gram_blocks = lax.map(block_gram, stacked) / count

    weight_blocks = weight.reshape(OUT, BLOCKS, BLK).transpose(1, 0, 2)
    level_table = [2.0, 4.0, 8.0, 128.0]

    def block_error(operands):
        block_piece, gram = operands
        values = block_piece.astype(jnp.float32)
        results = []
        for width_slot in range(4):
            levels = level_table[width_slot]
            delta = values - soft_quantize(values, levels)
            weighted = jnp.dot(delta, gram, precision=lax.Precision.HIGHEST)
            results.append(jnp.sum(weighted * delta) * (levels * levels / (OUT * BLK)))
        return jnp.stack(results)

    block_errors = lax.map(block_error, (weight_blocks, gram_blocks))

    per_panel = PANEL // BLK
    panels = D // PANEL
    weight_panels = weight.reshape(OUT, panels, PANEL).transpose(1, 0, 2)
    factor_panels = inv_chol.reshape(panels, per_panel, BLK, PANEL)
    level_panels = level_count(bit_widths).reshape(panels, per_panel)

    def panel_quant(operands):
        panel_weight, factor, levels = operands
        current = panel_weight.astype(jnp.float32)
        outputs = []
        for column_block in range(per_panel):
            first_column = column_block * BLK
            block_values = current[:, first_column:first_column + BLK]
            quantized_block = soft_quantize(block_values, levels[column_block])
            outputs.append(quantized_block.astype(jnp.bfloat16))
            if column_block + 1 < per_panel:
                factor_rows = factor[column_block]
                diagonal = jnp.diagonal(factor_rows[:, first_column:first_column + BLK])
                scaled_error = (block_values - quantized_block) / diagonal[None, :]
                update = jnp.dot(scaled_error, factor_rows[:, first_column + BLK:], precision=lax.Precision.HIGHEST)
                current = jnp.concatenate([current[:, :first_column + BLK], current[:, first_column + BLK:] - update], axis=1)
        return jnp.concatenate(outputs, axis=1)

    quantized = lax.map(panel_quant, (weight_panels, factor_panels, level_panels))
    quantized = quantized.transpose(1, 0, 2).reshape(OUT, D)
    return quantized, gram_blocks, block_errors
```

```python
import functools
import math

import jax
import jax.numpy as jnp
from jax import lax
from jax.experimental import pallas as pl
from jax.experimental.pallas import tpu as pltpu
from jax.sharding import PartitionSpec as P

BLK = 128
PANEL = 1024
PER = PANEL // BLK
PAIR = 2 * BLK

pad_token = 128004

SINE = (
    0.9999996039174559,
    -6.579691569594437,
    12.986435989563077,
    -12.18810142777418,
    6.5580417797975565,
    -1.9530312812214594,
)
MIB = 1024 * 1024


def sine_turn(r):
    square = r * r
    total = SINE[-1] * square + SINE[-2]
    for factor in SINE[-3::-1]:
        total = total * square + factor
    return r * total


def row_dot(a, b):
    return lax.dot_general(a, b, (((0,), (0,)), ((), ())), preferred_element_type=jnp.float32)


def dot(a, b):
    return jnp.dot(a, b, preferred_element_type=jnp.float32)


def gram_kernel(steps, x_ref, id_ref, out_ref):
    step = pl.program_id(0)
    live = jnp.where(id_ref[...] != pad_token, 1.0, 0.0).astype(jnp.float32)

    @pl.when(step < steps)
    def _():
        x = x_ref[...]
        masked = (x.astype(jnp.float32) * live).astype(x.dtype)
        whole = row_dot(masked, x)
        out_ref[0] = whole[:BLK, :BLK]
        out_ref[1] = whole[BLK:, BLK:]

    @pl.when(step == steps)
    def _():
        count = jnp.sum(live, axis=0, keepdims=True)
        out_ref[...] = jnp.broadcast_to(count[None], out_ref.shape)


def gram_sums(activations, token_ids):
    tokens, width = activations.shape
    steps = width // PAIR
    return pl.pallas_call(
        functools.partial(gram_kernel, steps),
        grid=(steps + 1,),
        in_specs=[
            pl.BlockSpec((tokens, PAIR), lambda i: (0, jnp.minimum(i, steps - 1))),
            pl.BlockSpec((tokens, 1), lambda i: (0, 0)),
        ],
        out_specs=pl.BlockSpec((2, BLK, BLK), lambda i: (i, 0, 0)),
        out_shape=jax.ShapeDtypeStruct((2 * steps + 2, BLK, BLK), jnp.float32),
        compiler_params=pltpu.CompilerParams(vmem_limit_bytes=32 * MIB),
        cost_estimate=pl.CostEstimate(
            flops=2 * tokens * width * PAIR, bytes_accessed=2 * tokens * width, transcendentals=0
        ),
        name="gram_sums",
    )(activations, token_ids.reshape(tokens, 1))


PI = math.pi


def clipped(smooth, levels):
    half = levels - 0.5
    return jnp.clip(smooth, -levels / half, (levels - 1.0) / half)


def block_deltas(piece):
    w = piece.astype(jnp.float32)
    largest = jnp.max(jnp.abs(w), axis=-1, keepdims=True) + 1e-6
    v = w * (1.0 / largest)
    sine = sine_turn(0.5 * v) * (2.0 * PI)
    square = sine * sine
    third = sine * ((-4.0 / (3.0 * PI)) * square + (3.0 / (3.0 * PI)))
    c = 1.0 / (7.0 * PI)
    seventh = sine * (((-64.0 * c * square + 112.0 * c) * square - 56.0 * c) * square + 7.0 * c)
    x2 = third * third
    k = (3.0 * PI) ** 2
    fifteenth = third * ((3.2 * k * k * x2 - 4.0 * k) * x2 + 1.0)
    turns = 127.5 * v
    last = sine_turn(turns - jnp.round(turns)) * (1.0 / 127.5)
    out = []
    for levels, term in ((2.0, third), (4.0, seventh), (8.0, fifteenth), (128.0, last)):
        out.append(((v - clipped(v - term, levels)) * largest).astype(jnp.bfloat16))
    return out


def error_kernel(rows, sub, w_ref, out_ref):
    @pl.when(pl.program_id(1) == 0)
    def _():
        out_ref[...] = jnp.zeros_like(out_ref)

    @pl.loop(0, w_ref.shape[1] // BLK)
    def _(block):
        columns = pl.ds(pl.multiple_of(block * BLK, BLK), BLK)
        first = second = None
        for start in range(0, rows, sub):
            pieces = [
                block_deltas(w_ref[pl.ds(at, 32), columns]) for at in range(start, start + sub, 32)
            ]
            e = [jnp.concatenate([p[i] for p in pieces], axis=0) for i in range(4)]
            low = jnp.concatenate(e[:2], axis=1)
            high = jnp.concatenate(e[2:], axis=1)
            a, b = row_dot(low, low), row_dot(high, high)
            first = a if first is None else first + a
            second = b if second is None else second + b
        out_ref[block, 0] += first[:BLK, :BLK]
        out_ref[block, 1] += first[BLK:, BLK:]
        out_ref[block, 2] += second[:BLK, :BLK]
        out_ref[block, 3] += second[BLK:, BLK:]


def error_products(weight, first_panel, panels):
    row_count, width = weight.shape[0], panels * PANEL
    rows = min(512, row_count)
    sub = 256
    return pl.pallas_call(
        functools.partial(error_kernel, rows, sub),
        grid=(width // PANEL, row_count // rows),
        in_specs=[pl.BlockSpec((rows, PANEL), lambda p, r: (r, p + first_panel))],
        out_specs=pl.BlockSpec((PER, 4, BLK, BLK), lambda p, r: (p, 0, 0, 0)),
        out_shape=jax.ShapeDtypeStruct((width // BLK, 4, BLK, BLK), jnp.float32),
        compiler_params=pltpu.CompilerParams(vmem_limit_bytes=32 * MIB),
        cost_estimate=pl.CostEstimate(
            flops=85 * row_count * width * PAIR,
            bytes_accessed=2 * row_count * width,
            transcendentals=0,
        ),
        name="error_products",
    )(weight)


def split(value):
    high = value.astype(jnp.bfloat16)
    return high, (value - high.astype(jnp.float32)).astype(jnp.bfloat16)


def quantize_block(current, levels):
    out, high, low = [], [], []
    for at in range(0, current.shape[0], 64):
        c = current[at : at + 64]
        largest = jnp.max(jnp.abs(c), axis=-1, keepdims=True) + 1e-6
        step = largest / (levels - 0.5)
        u = c * ((levels - 0.5) / largest)
        smooth = u - sine_turn(u - jnp.round(u))
        q = step * jnp.clip(smooth, -levels, levels - 1.0)
        out.append(q.astype(jnp.bfloat16))
        h, l = split(c - q)
        high.append(h)
        low.append(l)
    return tuple(jnp.concatenate(x, axis=0) for x in (out, high, low))


def panel_kernel(rows, streams, width_ref, w_ref, u_ref, out_ref, uh_ref, ul_ref, eh_ref, el_ref):
    panel = pl.program_id(0)

    @pl.when(pl.program_id(1) == 0)
    def _():
        for i in range(PER - 1):
            slot, first = (0, 0) if i == 0 else ((i, 0) if i < 4 else (7 - i, i * BLK))
            span = (PER - 1 - i) * BLK
            high, low = split(u_ref[0, slot, :, first : first + span])
            uh_ref[i * BLK : (i + 1) * BLK, (i + 1) * BLK :] = high
            ul_ref[i * BLK : (i + 1) * BLK, (i + 1) * BLK :] = low

    levels = []
    for j in range(PER):
        w = width_ref[panel * PER + j]
        levels.append(
            jnp.where(w == 2, 2.0, jnp.where(w == 3, 4.0, jnp.where(w == 4, 8.0, 128.0)))
        )
    part = rows // streams
    spans = [slice(s * part, (s + 1) * part) for s in range(streams)]
    for pair in range(PER // 2):
        left = slice(pair * PAIR, pair * PAIR + BLK)
        right = slice(pair * PAIR + BLK, (pair + 1) * PAIR)
        both = slice(pair * PAIR, (pair + 1) * PAIR)
        done = slice(0, pair * PAIR)
        current = []
        for span in spans:
            c = w_ref[span, both].astype(jnp.float32)
            if pair > 0:
                c = c - (
                    dot(eh_ref[span, done], uh_ref[done, both])
                    + dot(el_ref[span, done], uh_ref[done, both])
                    + dot(eh_ref[span, done], ul_ref[done, both])
                )
            current.append(c)
        halves = []
        for span, c in zip(spans, current):
            out, high, low = quantize_block(c[:, :BLK], levels[2 * pair])
            out_ref[span, left] = out
            halves.append((high, low))
        for span, c, (high, low) in zip(spans, current, halves):
            uh, ul = uh_ref[left, right], ul_ref[left, right]
            update = dot(
                jnp.concatenate([high, low], axis=1), jnp.concatenate([uh, uh], axis=0)
            ) + dot(high, ul)
            out, high2, low2 = quantize_block(c[:, BLK:] - update, levels[2 * pair + 1])
            out_ref[span, right] = out
            if pair + 1 < PER // 2:
                eh_ref[span, left] = high
                el_ref[span, left] = low
                eh_ref[span, right] = high2
                el_ref[span, right] = low2


def quantize_panels(weight, factor, bit_widths):
    row_count, width = weight.shape
    rows = min(512, row_count)
    kept = PANEL - PAIR
    return pl.pallas_call(
        functools.partial(panel_kernel, rows, 2),
        grid_spec=pltpu.PrefetchScalarGridSpec(
            num_scalar_prefetch=1,
            grid=(width // PANEL, row_count // rows),
            in_specs=[
                pl.BlockSpec((rows, PANEL), lambda p, r, s: (r, p)),
                pl.BlockSpec((1, PER // 2, BLK, PANEL - BLK), lambda p, r, s: (p, 0, 0, 0)),
            ],
            out_specs=pl.BlockSpec((rows, PANEL), lambda p, r, s: (r, p)),
            scratch_shapes=[
                pltpu.VMEM((PANEL, PANEL), jnp.bfloat16),
                pltpu.VMEM((PANEL, PANEL), jnp.bfloat16),
                pltpu.VMEM((rows, kept), jnp.bfloat16),
                pltpu.VMEM((rows, kept), jnp.bfloat16),
            ],
        ),
        out_shape=jax.ShapeDtypeStruct((row_count, width), jnp.bfloat16),
        compiler_params=pltpu.CompilerParams(vmem_limit_bytes=40 * MIB),
        cost_estimate=pl.CostEstimate(
            flops=40 * row_count * width * PAIR,
            bytes_accessed=4 * row_count * width,
            transcendentals=0,
        ),
        name="quantize_panels",
    )(bit_widths, weight, factor)


def scaled_rows(inv_chol):
    blocks, owned, width = inv_chol.shape
    panels = blocks // PER
    rows = inv_chol.reshape(panels, PER, owned, width)
    row = lax.broadcasted_iota(jnp.int32, (owned, BLK), 0) + lax.axis_index("dp") * owned
    mine = (lax.broadcasted_iota(jnp.int32, (owned, BLK), 1) == row)[None]
    parts = []
    for i in range(PER - 1):
        at = slice(i * BLK, (i + 1) * BLK)
        diagonal = jnp.sum(jnp.where(mine, rows[:, i, :, at], 0.0), axis=-1, keepdims=True)
        parts.append(rows[:, i, :, (i + 1) * BLK :] / diagonal)
    packed = [parts[0]] + [
        jnp.concatenate([parts[i], parts[PER - 1 - i]], axis=-1) for i in range(1, PER // 2)
    ]
    return jnp.stack(packed, axis=1)


def per_device(activations, token_ids, weight, inv_chol, bit_widths):
    blocks_here = weight.shape[1] // BLK
    out_rows = weight.shape[0] * lax.axis_size("dp")
    factor = lax.all_gather(scaled_rows(inv_chol), "dp", axis=2, tiled=True)
    partial = gram_sums(activations, token_ids)
    panels = weight.shape[1] // PANEL
    early = max(1, 3 * panels // 4)
    products = [error_products(weight, 0, early)]
    factor, partial, products[0], later_weight = lax.optimization_barrier(
        (factor, partial, products[0], weight)
    )
    gram_sum = lax.psum(partial, "dp")
    if early < panels:
        products.append(error_products(later_weight, early, panels - early))
    quantized = quantize_panels(later_weight, factor, bit_widths)
    gram_sum, quantized, *products = lax.optimization_barrier((gram_sum, quantized, *products))
    gram = gram_sum[:blocks_here] / gram_sum[blocks_here, 0, 0]
    owned = BLK // lax.axis_size("dp")
    gram_out = lax.dynamic_slice_in_dim(gram, lax.axis_index("dp") * owned, owned, 1)
    levels = jnp.array([2.0, 4.0, 8.0, 128.0], jnp.float32)
    sums, at = [], 0
    for part in products:
        sums.append(jnp.sum(part * gram[at : at + part.shape[0], None], axis=(2, 3)))
        at += part.shape[0]
    errors = jnp.concatenate(sums, axis=0) * (levels * levels / (out_rows * BLK))
    everywhere = jnp.zeros((blocks_here * lax.axis_size("tensor"), 4), jnp.float32)
    everywhere = lax.dynamic_update_slice(
        everywhere, errors, (lax.axis_index("tensor") * blocks_here, 0)
    )
    block_errors = lax.psum(everywhere, ("dp", "tensor"))
    return (quantized, gram_out, block_errors)


def solution(mesh):
    placed = (P("dp", "tensor"), P("dp"), P("dp", "tensor"), P("tensor", "dp", None), P("tensor"))
    return jax.shard_map(
        per_device,
        mesh=mesh,
        in_specs=placed,
        out_specs=(P("dp", "tensor"), P("tensor", "dp", None), P()),
        check_vma=False,
    )
```
